1024 devices in a mesh: dp: 64 (over y, z_lo, core), tensor: 16 (over x, z_hi).
Axes of the slice: x: 8, y: 8, z: 8 (z_hi: 2, z_lo: 4; z = z_hi * 4 + z_lo), core: 2. Of those that a mesh axis runs over, the one named last changes fastest.
Arguments:
- inputs: bfloat16 [24576, 6144], P('dp'), may hold values from -6 to 6
- ln_gain: float32 [6144], replicated, may hold values from 0.1 to 1.9
- w_query: bfloat16 [6144, 4096], P(None, 'tensor'), may hold values from -0.078125 to 0.078125
- query_grad: bfloat16 [24576, 4096], P('dp', 'tensor'), may hold values from -6 to 6
- skip_grad: bfloat16 [24576, 6144], P(('dp', 'tensor')), may hold values from -6 to 6
Outputs:
- input_grad: bfloat16 [24576, 6144], P(('dp', 'tensor'))
- weight_grad: float32 [6144, 4096], P('dp', 'tensor')
The draws below stay inside these ranges and needn't reach their ends.
All inputs are finite; a program needn't handle non-finite values.
Results may differ from the reference program's by a relative error of at most 0.015.
Values may be sent and summed in bfloat16 or wider, within the bound.
No kernel may reach another device: no remote copies, remote signals or barrier semaphores. Data moves between devices by JAX's collectives and lax.ppermute only.
A program may use at most 128 MiB of HBM per device.

```python
import jax
import jax.numpy as jnp
from jax import lax

D = 6144
HQ = 4096
TOKENS = 24576
N_DP = 64
N_TENSOR = 16


def level_of(own_key, dims, split, least, high):
    level = 1.0
    for position, blocks in split:
        steps = jax.random.uniform(jax.random.fold_in(jax.random.fold_in(own_key, 6), position), (blocks,), jnp.float32, least / len(split), high / len(split))
        level = level * jnp.repeat(jnp.exp(steps), dims[position] // blocks).reshape((-1,) + (1,) * (len(dims) - 1 - position))
    return level


def bell_draw(rng, extent, deviation, bound, cuts=(), dtype=jnp.bfloat16):
    entries = jax.random.normal(rng, extent, jnp.float32) * deviation
    if len(cuts) > 0:
        entries = level_of(rng, extent, cuts, -0.22, 0.18) * entries
    return jnp.clip(entries, min=-bound, max=bound).astype(dtype)


def setup_inputs(seed: int = 0) -> dict:
    streams_of = jax.random.split(jax.random.key(seed), 6)
    inputs = bell_draw(streams_of[0], (TOKENS, D), 1.0, 6.0, ((0, 64),))
    ln_gain = jnp.clip(1.0 + 0.18 * jax.random.normal(streams_of[1], (D,), jnp.float32), 0.1, 1.9)
    w_query = bell_draw(streams_of[2], (D, HQ), D ** -0.5, 0.078125, ((1, 16),))
    query_grad = bell_draw(streams_of[3], (TOKENS, HQ), 1.0, 6.0, ((0, 64), (1, 16)))
    skip_grad = bell_draw(streams_of[4], (TOKENS, D), 1.0, 6.0, ((0, 1024),))
    return {"inputs": inputs, "ln_gain": ln_gain, "w_query": w_query, "query_grad": query_grad, "skip_grad": skip_grad}


def reference(inputs, ln_gain, w_query, query_grad, skip_grad):
    hi = lax.Precision.HIGHEST
    values = inputs.astype(jnp.float32)
    center = values - lax.optimization_barrier(jnp.mean(values, axis=1, keepdims=True))
    inverse = lax.rsqrt(lax.optimization_barrier(jnp.mean(center * center, axis=1, keepdims=True)) + 1e-06)
    normed = center * inverse
    scaled = (normed * ln_gain[None, :]).astype(jnp.bfloat16)
    scaled_f = scaled.astype(jnp.float32)
    grads_f = query_grad.astype(jnp.float32)
    weight_grad = lax.dot_general(scaled_f, grads_f, (((0,), (0,)), ((), ())), precision=hi) / N_DP
    weights_f = w_query.astype(jnp.float32)
    group = grads_f.shape[1] // N_TENSOR

    def add_group(index, total):
        start = (index * group).astype(jnp.int32)
        part_g = lax.dynamic_slice_in_dim(grads_f, start, group, 1)
        part_w = lax.dynamic_slice_in_dim(weights_f, start, group, 1)
        term = lax.dot_general(part_g, part_w, (((1,), (1,)), ((), ())), precision=hi)
        return total + term.astype(jnp.bfloat16).astype(jnp.float32)
    d_scaled = lax.fori_loop(0, N_TENSOR, add_group, jnp.zeros(values.shape, jnp.float32))
    gated = d_scaled * ln_gain[None, :]
    mean_g = lax.optimization_barrier(jnp.mean(gated, axis=1, keepdims=True))
    mean_gn = lax.optimization_barrier(jnp.mean(gated * normed, axis=1, keepdims=True))
    input_grad = skip_grad.astype(jnp.float32) + inverse * (gated - mean_g - normed * mean_gn)
    return (input_grad.astype(jnp.bfloat16), weight_grad)
```

```python
import jax
import jax.numpy as jnp
from jax import lax
from jax.sharding import Mesh, PartitionSpec as P

DP = ("y", "z_lo", "core")
TENSOR = ("x", "z_hi")
SPLIT = (8, 4, 2, 8, 2)


def shifted(part, axis, step):
    size = lax.axis_size(axis)
    return lax.ppermute(part, axis, [(i, (i + step) % size) for i in range(size)])


def direct_reduce(blocks, axis):
    size = lax.axis_size(axis)
    me = lax.axis_index(axis)
    narrow = blocks.astype(jnp.bfloat16)
    arrived = [
        shifted(lax.dynamic_index_in_dim(narrow, (me + step) % size, 0, False), axis, step)
        for step in range(1, size)
    ]
    total = lax.dynamic_index_in_dim(blocks, me, 0, False)
    for part in arrived:
        total = total + part.astype(jnp.float32)
    return total


def weight_reduce(term):
    columns = term.shape[1]
    replicas = lax.axis_size(DP)
    cores, z_lo, y = lax.axis_size("core"), lax.axis_size("z_lo"), lax.axis_size("y")
    rows = term.shape[0] // replicas
    blocks = term.reshape(y * z_lo, cores, rows, columns).transpose(1, 0, 2, 3)
    total = direct_reduce(blocks, "core")
    total = direct_reduce(total.reshape(y, z_lo * rows, columns), "y")
    total = direct_reduce(total.reshape(z_lo, rows, columns), "z_lo")
    return total / replicas


def feature_reduce(query_grad, w_query):
    term = lax.dot_general(
        query_grad, w_query, (((1,), (1,)), ((), ())), preferred_element_type=jnp.float32
    ).astype(jnp.bfloat16)
    across = lax.psum_scatter(term, "x", scatter_dimension=0, tiled=True)
    halves = across.reshape(2, across.shape[0] // 2, across.shape[1])
    me = lax.axis_index("z_hi")
    own = lax.dynamic_index_in_dim(halves, me, 0, False)
    other = lax.dynamic_index_in_dim(halves, 1 - me, 0, False)
    return own.astype(jnp.float32) + shifted(other, "z_hi", 1).astype(jnp.float32)


def per_device(inputs, ln_gain, w_query, query_grad, skip_grad):
    d_scaled = feature_reduce(query_grad, w_query)
    values = inputs.astype(jnp.float32)
    mean = jnp.mean(values, axis=1, keepdims=True)
    center = values - mean
    inverse = lax.rsqrt(jnp.mean(center * center, axis=1, keepdims=True) + 1e-06)
    scaled = (center * inverse * ln_gain[None, :]).astype(jnp.bfloat16)
    term = lax.dot_general(
        scaled, query_grad, (((0,), (0,)), ((), ())), preferred_element_type=jnp.float32
    )
    weight_grad = weight_reduce(term)

    own_rows = skip_grad.shape[0]
    first = lax.axis_index(TENSOR) * own_rows
    own_values = lax.dynamic_slice_in_dim(inputs, first, own_rows, 0).astype(jnp.float32)
    mean_own = lax.dynamic_slice_in_dim(mean, first, own_rows, 0)
    inverse_own = lax.dynamic_slice_in_dim(inverse, first, own_rows, 0)
    normed_own = (own_values - mean_own) * inverse_own
    gated = d_scaled * ln_gain[None, :]
    mean_g = jnp.mean(gated, axis=1, keepdims=True)
    mean_gn = jnp.mean(gated * normed_own, axis=1, keepdims=True)
    input_grad = skip_grad.astype(jnp.float32) + inverse_own * (
        gated - mean_g - normed_own * mean_gn
    )
    return (input_grad.astype(jnp.bfloat16), weight_grad)


def solution(mesh):
    fine = Mesh(mesh.devices.reshape(SPLIT), DP + TENSOR)
    placed = (P(DP, None), P(), P(None, TENSOR), P(DP, TENSOR), P(DP + TENSOR, None))
    return jax.shard_map(
        per_device,
        mesh=fine,
        in_specs=placed,
        out_specs=(P(DP + TENSOR, None), P(DP, TENSOR)),
        check_vma=False,
    )
```

```python
import jax
import jax.numpy as jnp
from jax import lax
from jax.sharding import Mesh, PartitionSpec as P

DP = ("y", "z_lo", "core")
TENSOR = ("x", "z_hi")
SPLIT = (8, 4, 2, 8, 2)


def wide(part):
    return part.astype(jnp.float32)


def narrow(part):
    return part.astype(jnp.bfloat16)


def swap(part, axis, bit):
    return lax.ppermute(part, axis, [(i, i ^ bit) for i in range(lax.axis_size(axis))])


def swap_even(part, axis):
    return swap(part, axis, 1)


def swap_odd(part, axis):
    size = lax.axis_size(axis)
    return lax.ppermute(
        part, axis, [(i, (i + 1 if i % 2 else i - 1) % size) for i in range(size)]
    )


def halve(total, axis, bit, dim):
    mine = (lax.axis_index(axis) // bit) % 2
    send = lax.dynamic_index_in_dim(total, 1 - mine, dim, False)
    keep = lax.dynamic_index_in_dim(total, mine, dim, False)
    return wide(keep) + wide(swap(narrow(send), axis, bit))


def weight_reduce(term):
    replicas = lax.axis_size(DP)
    rows, columns = term.shape[0] // replicas, term.shape[1]
    total = term.reshape((2,) * 6 + (rows, columns))
    total = halve(total, "core", 1, 5)
    total = halve(total, "y", 1, 2)
    total = halve(total, "z_lo", 1, 3)
    total = halve(total, "z_lo", 2, 2)
    total = halve(total, "y", 2, 1)
    total = halve(total, "y", 4, 0)
    return total / replicas


def product(query_grad, w_query):
    return narrow(
        lax.dot_general(
            query_grad, w_query, (((1,), (1,)), ((), ())), preferred_element_type=jnp.float32
        )
    )


def feature_reduce(query_grad, w_query):
    size, sets = lax.axis_size("x"), lax.axis_size("z_hi")
    far = size // 2
    rows = query_grad.shape[0] // (size * sets)
    x, z_hi = lax.axis_index("x"), lax.axis_index("z_hi")
    parity = x % 2
    way = 1 - 2 * parity
    chunk = lax.dynamic_slice_in_dim(query_grad, (x + far) % size * (sets * rows), sets * rows, 0)
    first = product(chunk, w_query).reshape(sets, rows, -1)
    first, query_grad = lax.optimization_barrier((first, query_grad))
    one = swap_even(lax.dynamic_index_in_dim(first, parity, 0, False), "x")
    two = swap_odd(lax.dynamic_index_in_dim(first, 1 - parity, 0, False), "x")
    terms = product(query_grad, w_query).reshape(size, sets, rows, -1)

    def term(step):
        return wide(lax.dynamic_index_in_dim(terms, (x + step + size) % size, 0, False))

    which = jnp.arange(sets)[:, None, None]
    one = jnp.where(which == 1 - parity, one[None], jnp.bfloat16(0))
    two = jnp.where(which == parity, two[None], jnp.bfloat16(0))
    for step in range(far - 1, 0, -1):
        up = narrow(term(way * step) + wide(two))
        down = narrow(term(-way * step) + wide(one))
        up, down = lax.optimization_barrier((up, down))
        one, two = swap_even(up, "x"), swap_odd(down, "x")
    total = term(0) + wide(one) + wide(two)
    own = lax.dynamic_index_in_dim(total, z_hi, 0, False)
    other = lax.dynamic_index_in_dim(total, 1 - z_hi, 0, False)
    return own + wide(swap(narrow(other), "z_hi", 1))


def per_device(inputs, ln_gain, w_query, query_grad, skip_grad):
    d_scaled = feature_reduce(query_grad, w_query)
    values = inputs.astype(jnp.float32)
    mean = jnp.mean(values, axis=1, keepdims=True)
    center = values - mean
    inverse = lax.rsqrt(jnp.mean(center * center, axis=1, keepdims=True) + 1e-06)
    scaled = (center * inverse * ln_gain[None, :]).astype(jnp.bfloat16)
    weight_grad = weight_reduce(
        narrow(
            lax.dot_general(
                scaled, query_grad, (((0,), (0,)), ((), ())), preferred_element_type=jnp.float32
            )
        )
    )

    own_rows = skip_grad.shape[0]
    first = lax.axis_index(TENSOR) * own_rows
    own_values = lax.dynamic_slice_in_dim(inputs, first, own_rows, 0).astype(jnp.float32)
    mean_own = lax.dynamic_slice_in_dim(mean, first, own_rows, 0)
    inverse_own = lax.dynamic_slice_in_dim(inverse, first, own_rows, 0)
    normed_own = (own_values - mean_own) * inverse_own
    gated = d_scaled * ln_gain[None, :]
    mean_g = jnp.mean(gated, axis=1, keepdims=True)
    mean_gn = jnp.mean(gated * normed_own, axis=1, keepdims=True)
    input_grad = skip_grad.astype(jnp.float32) + inverse_own * (
        gated - mean_g - normed_own * mean_gn
    )
    return (input_grad.astype(jnp.bfloat16), weight_grad)


def solution(mesh):
    fine = Mesh(mesh.devices.reshape(SPLIT), DP + TENSOR)
    placed = (P(DP, None), P(), P(None, TENSOR), P(DP, TENSOR), P(DP + TENSOR, None))
    return jax.shard_map(
        per_device,
        mesh=fine,
        in_specs=placed,
        out_specs=(P(DP + TENSOR, None), P(DP, TENSOR)),
        check_vma=False,
    )
```

```python
import jax
import jax.numpy as jnp
from jax import lax
from jax.sharding import Mesh, PartitionSpec as P

DP = ("y", "z_lo", "core")
TENSOR = ("x", "z_hi")
SPLIT = (8, 4, 2, 8, 2)


def shifted(part, axis, step):
    size = lax.axis_size(axis)
    return lax.ppermute(part, axis, [(i, (i + step) % size) for i in range(size)])


def weight_reduce(term):
    replicas, cores = lax.axis_size(DP), lax.axis_size("core")
    rows, columns = term.shape[0] // replicas, term.shape[1]
    blocks = term.astype(jnp.bfloat16).reshape(replicas // cores, cores, rows, columns)
    me = lax.axis_index("core")
    own = lax.dynamic_index_in_dim(blocks, me, 1, False)
    other = lax.dynamic_index_in_dim(blocks, 1 - me, 1, False)
    pair = own.astype(jnp.float32) + shifted(other, "core", 1).astype(jnp.float32)
    parts = lax.all_to_all(pair.astype(jnp.bfloat16), ("y", "z_lo"), 0, 0, tiled=True)
    return jnp.sum(parts.astype(jnp.float32), axis=0) / replicas


def feature_reduce(query_grad, w_query):
    term = lax.dot_general(
        query_grad, w_query, (((1,), (1,)), ((), ())), preferred_element_type=jnp.float32
    ).astype(jnp.bfloat16)
    across = lax.psum_scatter(term, "x", scatter_dimension=0, tiled=True)
    halves = across.reshape(2, across.shape[0] // 2, across.shape[1])
    me = lax.axis_index("z_hi")
    own = lax.dynamic_index_in_dim(halves, me, 0, False)
    other = lax.dynamic_index_in_dim(halves, 1 - me, 0, False)
    return own.astype(jnp.float32) + shifted(other, "z_hi", 1).astype(jnp.float32)


def per_device(inputs, ln_gain, w_query, query_grad, skip_grad):
    d_scaled = feature_reduce(query_grad, w_query)
    values = inputs.astype(jnp.float32)
    mean = jnp.mean(values, axis=1, keepdims=True)
    center = values - mean
    inverse = lax.rsqrt(jnp.mean(center * center, axis=1, keepdims=True) + 1e-06)
    scaled = (center * inverse * ln_gain[None, :]).astype(jnp.bfloat16)
    term = lax.dot_general(
        scaled, query_grad, (((0,), (0,)), ((), ())), preferred_element_type=jnp.float32
    )
    weight_grad = weight_reduce(term)

    own_rows = skip_grad.shape[0]
    first = lax.axis_index(TENSOR) * own_rows
    own_values = lax.dynamic_slice_in_dim(inputs, first, own_rows, 0).astype(jnp.float32)
    mean_own = lax.dynamic_slice_in_dim(mean, first, own_rows, 0)
    inverse_own = lax.dynamic_slice_in_dim(inverse, first, own_rows, 0)
    normed_own = (own_values - mean_own) * inverse_own
    gated = d_scaled * ln_gain[None, :]
    mean_g = jnp.mean(gated, axis=1, keepdims=True)
    mean_gn = jnp.mean(gated * normed_own, axis=1, keepdims=True)
    input_grad = skip_grad.astype(jnp.float32) + inverse_own * (
        gated - mean_g - normed_own * mean_gn
    )
    return (input_grad.astype(jnp.bfloat16), weight_grad)


def solution(mesh):
    fine = Mesh(mesh.devices.reshape(SPLIT), DP + TENSOR)
    placed = (P(DP, None), P(), P(None, TENSOR), P(DP, TENSOR), P(DP + TENSOR, None))
    return jax.shard_map(
        per_device,
        mesh=fine,
        in_specs=placed,
        out_specs=(P(DP + TENSOR, None), P(DP, TENSOR)),
        check_vma=False,
    )
```

```python
import jax
import jax.numpy as jnp
from jax import lax
from jax.sharding import Mesh, PartitionSpec as P

DP = ("y", "z_lo", "core")
TENSOR = ("x", "z_hi")
SPLIT = (8, 4, 2, 8, 2)


def wide(part):
    return part.astype(jnp.float32)


def narrow(part):
    return part.astype(jnp.bfloat16)


def swap(part, axis, bit):
    return lax.ppermute(part, axis, [(i, i ^ bit) for i in range(lax.axis_size(axis))])


def swap_even(part, axis):
    return swap(part, axis, 1)


def swap_odd(part, axis):
    size = lax.axis_size(axis)
    return lax.ppermute(
        part, axis, [(i, (i + 1 if i % 2 else i - 1) % size) for i in range(size)]
    )


def pair_blocks(term):
    cores, rows = lax.axis_size("core"), term.shape[0] // lax.axis_size(DP)
    return term.reshape(-1, cores, rows, term.shape[1])


def core_sum(blocks):
    me = lax.axis_index("core")
    own = lax.dynamic_index_in_dim(blocks, me, 1, False)
    other = lax.dynamic_index_in_dim(blocks, 1 - me, 1, False)
    return narrow(wide(own) + wide(swap(other, "core", 1)))


def weight_reduce(pair):
    parts = lax.all_to_all(pair, ("y", "z_lo"), 0, 0, tiled=True)
    return jnp.sum(wide(parts), axis=0) / lax.axis_size(DP)


def product(query_grad, w_query):
    return narrow(
        lax.dot_general(
            query_grad, w_query, (((1,), (1,)), ((), ())), preferred_element_type=jnp.float32
        )
    )


def across(part, even):
    size, sets = lax.axis_size("x"), lax.axis_size("z_hi")
    moves = []
    for i in range(size):
        to = (i + (1 if (i % 2 == 0) == even else -1)) % size
        moves += [(i * sets + j, to * sets + 1 - j) for j in range(sets)]
    return lax.ppermute(part, TENSOR, moves)


def feature_reduce(query_grad, w_query, weight_term):
    size, sets = lax.axis_size("x"), lax.axis_size("z_hi")
    far = size // 2
    rows = query_grad.shape[0] // (size * sets)
    x, z_hi = lax.axis_index("x"), lax.axis_index("z_hi")
    parity = x % 2
    way = 1 - 2 * parity
    chunk = lax.dynamic_slice_in_dim(query_grad, (x + far) % size * (sets * rows), sets * rows, 0)
    first = product(chunk, w_query).reshape(sets, rows, -1)
    first, query_grad = lax.optimization_barrier((first, query_grad))
    one = swap_even(lax.dynamic_index_in_dim(first, parity, 0, False), "x")
    two = swap_odd(lax.dynamic_index_in_dim(first, 1 - parity, 0, False), "x")
    terms = product(query_grad, w_query).reshape(size, sets, rows, -1)
    blocks = pair_blocks(weight_term(query_grad))

    def term(step):
        return lax.dynamic_index_in_dim(terms, (x + step + size) % size, 0, False)

    def pick(parts, index):
        return lax.dynamic_index_in_dim(parts, index, 0, False)

    which = jnp.arange(sets)[:, None, None]
    one = jnp.where(which == 1 - parity, one[None], jnp.bfloat16(0))
    two = jnp.where(which == parity, two[None], jnp.bfloat16(0))
    for step in range(far - 1, 1, -1):
        up = narrow(wide(term(way * step)) + wide(two))
        down = narrow(wide(term(-way * step)) + wide(one))
        if step == far - 1:
            up, down, blocks = lax.optimization_barrier((up, down, blocks))
        else:
            up, down = lax.optimization_barrier((up, down))
        one, two = swap_even(up, "x"), swap_odd(down, "x")
        if step == far - 1:
            pair = core_sum(blocks)
            one, two, _ = lax.optimization_barrier((one, two, pair))
            beside = swap(pick(term(0), 1 - z_hi), "z_hi", 1)
    ups, downs = wide(term(way)) + wide(two), wide(term(-way)) + wide(one)
    parts = lax.optimization_barrier(
        tuple(narrow(pick(p, index)) for index in (1 - z_hi, z_hi) for p in (ups, downs))
    )
    arrived = (
        across(parts[0], True),
        across(parts[1], False),
        swap_even(parts[2], "x"),
        swap_odd(parts[3], "x"),
        beside,
    )
    return sum((wide(part) for part in arrived), wide(pick(term(0), z_hi))), pair


def per_device(inputs, ln_gain, w_query, query_grad, skip_grad):
    values = inputs.astype(jnp.float32)
    mean = jnp.mean(values, axis=1, keepdims=True)
    center = values - mean
    inverse = lax.rsqrt(jnp.mean(center * center, axis=1, keepdims=True) + 1e-06)
    scaled = (center * inverse * ln_gain[None, :]).astype(jnp.bfloat16)

    def weight_term(grads):
        return narrow(
            lax.dot_general(
                scaled, grads, (((0,), (0,)), ((), ())), preferred_element_type=jnp.float32
            )
        )

    d_scaled, pair = feature_reduce(query_grad, w_query, weight_term)
    weight_grad = weight_reduce(pair)

    own_rows = skip_grad.shape[0]
    first = lax.axis_index(TENSOR) * own_rows
    own_values = lax.dynamic_slice_in_dim(inputs, first, own_rows, 0).astype(jnp.float32)
    mean_own = lax.dynamic_slice_in_dim(mean, first, own_rows, 0)
    inverse_own = lax.dynamic_slice_in_dim(inverse, first, own_rows, 0)
    normed_own = (own_values - mean_own) * inverse_own
    gated = d_scaled * ln_gain[None, :]
    mean_g = jnp.mean(gated, axis=1, keepdims=True)
    mean_gn = jnp.mean(gated * normed_own, axis=1, keepdims=True)
    input_grad = skip_grad.astype(jnp.float32) + inverse_own * (
        gated - mean_g - normed_own * mean_gn
    )
    return (input_grad.astype(jnp.bfloat16), weight_grad)


def solution(mesh):
    fine = Mesh(mesh.devices.reshape(SPLIT), DP + TENSOR)
    placed = (P(DP, None), P(), P(None, TENSOR), P(DP, TENSOR), P(DP + TENSOR, None))
    return jax.shard_map(
        per_device,
        mesh=fine,
        in_specs=placed,
        out_specs=(P(DP + TENSOR, None), P(DP, TENSOR)),
        check_vma=False,
    )
```

```python
import jax
import jax.numpy as jnp
from jax import lax
from jax.experimental import pallas as pl
from jax.experimental.pallas import tpu as pltpu
from jax.sharding import Mesh, PartitionSpec as P

DP = ("y", "z_lo", "core")
TENSOR = ("x", "z_hi")
SPLIT = (8, 4, 2, 8, 2)


def shifted(part, axis, step):
    size = lax.axis_size(axis)
    return lax.ppermute(part, axis, [(i, (i + step) % size) for i in range(size)])


def weight_reduce(term):
    replicas, cores = lax.axis_size(DP), lax.axis_size("core")
    rows, columns = term.shape[0] // replicas, term.shape[1]
    blocks = term.astype(jnp.bfloat16).reshape(replicas // cores, cores, rows, columns)
    me = lax.axis_index("core")
    own = lax.dynamic_index_in_dim(blocks, me, 1, False)
    other = lax.dynamic_index_in_dim(blocks, 1 - me, 1, False)
    pair = own.astype(jnp.float32) + shifted(other, "core", 1).astype(jnp.float32)
    parts = lax.all_to_all(pair.astype(jnp.bfloat16), ("y", "z_lo"), 0, 0, tiled=True)
    return jnp.sum(parts.astype(jnp.float32), axis=0) / replicas


def product_kernel(grads_ref, weights_ref, out_ref):
    out_ref[...] = lax.dot_general(
        grads_ref[...],
        weights_ref[...],
        (((1,), (1,)), ((), ())),
        preferred_element_type=jnp.float32,
    ).astype(out_ref.dtype)


def product(query_grad, w_query):
    rows, depth = query_grad.shape
    features = w_query.shape[0]
    block = features // 6
    return pl.pallas_call(
        product_kernel,
        grid=(features // block,),
        in_specs=[
            pl.BlockSpec((rows, depth), lambda i: (0, 0)),
            pl.BlockSpec((block, depth), lambda i: (i, 0)),
        ],
        out_specs=pl.BlockSpec((rows, block), lambda i: (0, i)),
        out_shape=jax.ShapeDtypeStruct((rows, features), jnp.bfloat16),
        compiler_params=pltpu.CompilerParams(vmem_limit_bytes=60 << 20),
        cost_estimate=pl.CostEstimate(
            flops=2 * rows * depth * features,
            bytes_accessed=2 * (rows * depth + features * depth + rows * features),
            transcendentals=0,
        ),
    )(query_grad, w_query)


def finish_kernel(
    place_ref, sums_ref, arrived_ref, inputs_ref, skip_ref, gain_ref, out_ref
):
    del place_ref
    values = inputs_ref[0].astype(jnp.float32)
    center = values - jnp.mean(values, axis=1, keepdims=True)
    inverse = lax.rsqrt(jnp.mean(center * center, axis=1, keepdims=True) + 1e-06)
    normed = center * inverse
    summed = sums_ref[0].astype(jnp.float32) + arrived_ref[...].astype(jnp.float32)
    gated = summed * gain_ref[...]
    mean_g = jnp.mean(gated, axis=1, keepdims=True)
    mean_gn = jnp.mean(gated * normed, axis=1, keepdims=True)
    grad = skip_ref[...].astype(jnp.float32) + inverse * (gated - mean_g - normed * mean_gn)
    out_ref[...] = grad.astype(out_ref.dtype)


def finish(sums, arrived, inputs, skip_grad, ln_gain):
    rows, features = skip_grad.shape
    place = jnp.stack([lax.axis_index("z_hi"), lax.axis_index(TENSOR)]).astype(jnp.int32)
    whole = pl.BlockSpec((rows, features), lambda i, place: (0, 0))
    return pl.pallas_call(
        finish_kernel,
        grid_spec=pltpu.PrefetchScalarGridSpec(
            num_scalar_prefetch=1,
            grid=(1,),
            in_specs=[
                pl.BlockSpec((1, rows, features), lambda i, place: (place[0], 0, 0)),
                whole,
                pl.BlockSpec((1, rows, features), lambda i, place: (place[1], 0, 0)),
                whole,
                pl.BlockSpec((1, features), lambda i, place: (0, 0)),
            ],
            out_specs=whole,
        ),
        out_shape=jax.ShapeDtypeStruct(skip_grad.shape, jnp.bfloat16),
        compiler_params=pltpu.CompilerParams(vmem_limit_bytes=60 << 20),
    )(
        place,
        sums,
        arrived,
        inputs.reshape(-1, rows, features),
        skip_grad,
        ln_gain.reshape(1, features),
    )


def per_device(inputs, ln_gain, w_query, query_grad, skip_grad):
    term = product(query_grad, w_query)
    across = lax.psum_scatter(term, "x", scatter_dimension=0, tiled=True)
    sums = across.reshape(2, across.shape[0] // 2, across.shape[1])
    other = lax.dynamic_index_in_dim(sums, 1 - lax.axis_index("z_hi"), 0, False)
    arrived = shifted(other, "z_hi", 1)

    values = inputs.astype(jnp.float32)
    center = values - jnp.mean(values, axis=1, keepdims=True)
    inverse = lax.rsqrt(jnp.mean(center * center, axis=1, keepdims=True) + 1e-06)
    scaled = (center * inverse * ln_gain[None, :]).astype(jnp.bfloat16)
    weight_grad = weight_reduce(
        lax.dot_general(
            scaled, query_grad, (((0,), (0,)), ((), ())), preferred_element_type=jnp.float32
        )
    )
    input_grad = finish(sums, arrived, inputs, skip_grad, ln_gain)
    return (input_grad, weight_grad)


def solution(mesh):
    fine = Mesh(mesh.devices.reshape(SPLIT), DP + TENSOR)
    placed = (P(DP, None), P(), P(None, TENSOR), P(DP, TENSOR), P(DP + TENSOR, None))
    return jax.shard_map(
        per_device,
        mesh=fine,
        in_specs=placed,
        out_specs=(P(DP + TENSOR, None), P(DP, TENSOR)),
        check_vma=False,
    )
```

```python
import jax
import jax.numpy as jnp
from jax import lax
from jax.experimental import pallas as pl
from jax.experimental.pallas import tpu as pltpu
from jax.sharding import Mesh, PartitionSpec as P

DP = ("y", "z_lo", "core")
TENSOR = ("x", "z_hi")
SPLIT = (8, 4, 2, 8, 2)


def shifted(part, axis, step):
    size = lax.axis_size(axis)
    return lax.ppermute(part, axis, [(i, (i + step) % size) for i in range(size)])


def core_sum(term):
    replicas, cores = lax.axis_size(DP), lax.axis_size("core")
    rows, columns = term.shape[0] // replicas, term.shape[1]
    blocks = term.astype(jnp.bfloat16).reshape(replicas // cores, cores, rows, columns)
    me = lax.axis_index("core")
    own = lax.dynamic_index_in_dim(blocks, me, 1, False)
    other = lax.dynamic_index_in_dim(blocks, 1 - me, 1, False)
    pair = own.astype(jnp.float32) + shifted(other, "core", 1).astype(jnp.float32)
    return pair.astype(jnp.bfloat16)


def weight_reduce(pair):
    parts = lax.all_to_all(pair, ("y", "z_lo"), 0, 0, tiled=True)
    return jnp.sum(parts.astype(jnp.float32), axis=0) / lax.axis_size(DP)


PIECES = 4
DIRECT = 1024


def product_kernel(grads_hbm, weights_hbm, out_hbm, grads, weights, out, took, loaded, stored):
    pieces, block = weights.shape[:2]
    first = pltpu.make_async_copy(grads_hbm, grads, took)
    first.start()
    loads = []
    for i in range(pieces):
        load = pltpu.make_async_copy(
            weights_hbm.at[pl.ds(i * block, block)], weights.at[i], loaded.at[i]
        )
        load.start()
        loads.append(load)
    first.wait()
    stores = []
    for i in range(pieces):
        loads[i].wait()
        out[i] = lax.dot_general(
            grads[...],
            weights[i],
            (((1,), (1,)), ((), ())),
            preferred_element_type=jnp.float32,
        ).astype(out.dtype)
        store = pltpu.make_async_copy(
            out.at[i], out_hbm.at[:, pl.ds(i * block, block)], stored.at[i]
        )
        store.start()
        stores.append(store)
    for store in stores:
        store.wait()


def product(query_grad, w_query, features):
    rows, depth = query_grad.shape
    block = features // PIECES
    return pl.pallas_call(
        product_kernel,
        in_specs=[pl.BlockSpec(memory_space=pl.ANY)] * 2,
        out_specs=pl.BlockSpec(memory_space=pl.ANY),
        out_shape=jax.ShapeDtypeStruct((rows, features), jnp.bfloat16),
        scratch_shapes=[
            pltpu.VMEM((rows, depth), jnp.bfloat16),
            pltpu.VMEM((PIECES, block, depth), jnp.bfloat16),
            pltpu.VMEM((PIECES, rows, block), jnp.bfloat16),
            pltpu.SemaphoreType.DMA,
            pltpu.SemaphoreType.DMA((PIECES,)),
            pltpu.SemaphoreType.DMA((PIECES,)),
        ],
        compiler_params=pltpu.CompilerParams(vmem_limit_bytes=60 << 20),
        cost_estimate=pl.CostEstimate(
            flops=2 * rows * depth * features,
            bytes_accessed=2 * (rows * depth + features * depth + rows * features),
            transcendentals=0,
        ),
    )(query_grad, w_query)


def finish_kernel(
    place_ref, sums_ref, arrived_ref, direct_ref, inputs_ref, skip_ref, gain_ref, out_ref
):
    del place_ref
    values = inputs_ref[0].astype(jnp.float32)
    center = values - jnp.mean(values, axis=1, keepdims=True)
    inverse = lax.rsqrt(jnp.mean(center * center, axis=1, keepdims=True) + 1e-06)
    normed = center * inverse
    summed = sums_ref[0].astype(jnp.float32) + arrived_ref[...].astype(jnp.float32)
    gated = jnp.concatenate([summed, direct_ref[...]], axis=1) * gain_ref[...]
    mean_g = jnp.mean(gated, axis=1, keepdims=True)
    mean_gn = jnp.mean(gated * normed, axis=1, keepdims=True)
    grad = skip_ref[...].astype(jnp.float32) + inverse * (gated - mean_g - normed * mean_gn)
    out_ref[...] = grad.astype(out_ref.dtype)


def finish(sums, arrived, direct, inputs, skip_grad, ln_gain):
    rows, features = skip_grad.shape
    ringed = sums.shape[2]
    place = jnp.stack([lax.axis_index("z_hi"), lax.axis_index(TENSOR)]).astype(jnp.int32)
    whole = pl.BlockSpec((rows, features), lambda i, place: (0, 0))
    return pl.pallas_call(
        finish_kernel,
        grid_spec=pltpu.PrefetchScalarGridSpec(
            num_scalar_prefetch=1,
            grid=(1,),
            in_specs=[
                pl.BlockSpec((1, rows, ringed), lambda i, place: (place[0], 0, 0)),
                pl.BlockSpec((rows, ringed), lambda i, place: (0, 0)),
                pl.BlockSpec((rows, features - ringed), lambda i, place: (0, 0)),
                pl.BlockSpec((1, rows, features), lambda i, place: (place[1], 0, 0)),
                whole,
                pl.BlockSpec((1, features), lambda i, place: (0, 0)),
            ],
            out_specs=whole,
        ),
        out_shape=jax.ShapeDtypeStruct(skip_grad.shape, jnp.bfloat16),
        compiler_params=pltpu.CompilerParams(vmem_limit_bytes=60 << 20),
    )(
        place,
        sums,
        arrived,
        direct,
        inputs.reshape(-1, rows, features),
        skip_grad,
        ln_gain.reshape(1, features),
    )


def per_device(inputs, ln_gain, w_query, query_grad, skip_grad):
    rows, features = skip_grad.shape
    ringed = features - DIRECT
    term = product(query_grad, w_query, ringed)
    across = lax.psum_scatter(term, "x", scatter_dimension=0, tiled=True)
    sums = across.reshape(2, rows, ringed)
    other = lax.dynamic_index_in_dim(sums, 1 - lax.axis_index("z_hi"), 0, False)
    arrived = shifted(other, "z_hi", 1)

    values = inputs.astype(jnp.float32)
    center = values - jnp.mean(values, axis=1, keepdims=True)
    inverse = lax.rsqrt(jnp.mean(center * center, axis=1, keepdims=True) + 1e-06)
    scaled = (center * inverse * ln_gain[None, :]).astype(jnp.bfloat16)
    pair = core_sum(
        lax.dot_general(
            scaled, query_grad, (((0,), (0,)), ((), ())), preferred_element_type=jnp.float32
        )
    )
    blocks = (
        lax.dot_general(
            query_grad,
            w_query[ringed:],
            (((1,), (1,)), ((), ())),
            preferred_element_type=jnp.float32,
        )
        .astype(jnp.bfloat16)
        .reshape(-1, rows, DIRECT)
    )
    pair, blocks = lax.optimization_barrier((pair, blocks))
    weight_grad = weight_reduce(pair)
    parts = lax.all_to_all(blocks, TENSOR, 0, 0, tiled=True)
    direct = jnp.sum(parts.astype(jnp.float32), axis=0)
    input_grad = finish(sums, arrived, direct, inputs, skip_grad, ln_gain)
    return (input_grad, weight_grad)


def solution(mesh):
    fine = Mesh(mesh.devices.reshape(SPLIT), DP + TENSOR)
    placed = (P(DP, None), P(), P(None, TENSOR), P(DP, TENSOR), P(DP + TENSOR, None))
    return jax.shard_map(
        per_device,
        mesh=fine,
        in_specs=placed,
        out_specs=(P(DP + TENSOR, None), P(DP, TENSOR)),
        check_vma=False,
    )
```

```python
import jax
import jax.numpy as jnp
from jax import lax
from jax.experimental import pallas as pl
from jax.experimental.pallas import tpu as pltpu
from jax.sharding import Mesh, PartitionSpec as P

DP = ("y", "z_lo", "core")
TENSOR = ("x", "z_hi")
SPLIT = (8, 4, 2, 8, 2)


def shifted(part, axis, step):
    size = lax.axis_size(axis)
    return lax.ppermute(part, axis, [(i, (i + step) % size) for i in range(size)])


def core_sum(term):
    rows, columns = term.shape[0] // lax.axis_size(DP), term.shape[1]
    sizes = [lax.axis_size(axis) for axis in DP]
    blocks = term.astype(jnp.bfloat16).reshape(*sizes, rows, columns)
    me = lax.axis_index("core")
    own = lax.dynamic_index_in_dim(blocks, me, 2, False)
    other = lax.dynamic_index_in_dim(blocks, 1 - me, 2, False)
    pair = own.astype(jnp.float32) + shifted(other, "core", 1).astype(jnp.float32)
    return pair.astype(jnp.bfloat16).swapaxes(0, 1)


def exchange(total, axis):
    return jnp.sum(lax.all_to_all(total, axis, 0, 0, tiled=True).astype(jnp.float32), axis=0)


PIECES = 4


def product_kernel(grads_hbm, weights_hbm, out_hbm, grads, weights, out, took, loaded, stored):
    pieces, block = weights.shape[:2]
    first = pltpu.make_async_copy(grads_hbm, grads, took)
    first.start()
    loads = []
    for i in range(pieces):
        load = pltpu.make_async_copy(
            weights_hbm.at[pl.ds(i * block, block)], weights.at[i], loaded.at[i]
        )
        load.start()
        loads.append(load)
    first.wait()
    stores = []
    for i in range(pieces):
        loads[i].wait()
        out[i] = lax.dot_general(
            grads[...],
            weights[i],
            (((1,), (1,)), ((), ())),
            preferred_element_type=jnp.float32,
        ).astype(out.dtype)
        store = pltpu.make_async_copy(
            out.at[i], out_hbm.at[:, pl.ds(i * block, block)], stored.at[i]
        )
        store.start()
        stores.append(store)
    for store in stores:
        store.wait()


def product(query_grad, w_query, features):
    rows, depth = query_grad.shape
    block = features // PIECES
    return pl.pallas_call(
        product_kernel,
        in_specs=[pl.BlockSpec(memory_space=pl.ANY)] * 2,
        out_specs=pl.BlockSpec(memory_space=pl.ANY),
        out_shape=jax.ShapeDtypeStruct((rows, features), jnp.bfloat16),
        scratch_shapes=[
            pltpu.VMEM((rows, depth), jnp.bfloat16),
            pltpu.VMEM((PIECES, block, depth), jnp.bfloat16),
            pltpu.VMEM((PIECES, rows, block), jnp.bfloat16),
            pltpu.SemaphoreType.DMA,
            pltpu.SemaphoreType.DMA((PIECES,)),
            pltpu.SemaphoreType.DMA((PIECES,)),
        ],
        compiler_params=pltpu.CompilerParams(vmem_limit_bytes=60 << 20),
        cost_estimate=pl.CostEstimate(
            flops=2 * rows * depth * features,
            bytes_accessed=2 * (rows * depth + features * depth + rows * features),
            transcendentals=0,
        ),
    )(query_grad, w_query)


def per_device(inputs, ln_gain, w_query, query_grad, skip_grad):
    own_rows, features = skip_grad.shape
    term = product(query_grad, w_query, features)
    across = lax.psum_scatter(term, "x", scatter_dimension=0, tiled=True)

    values = inputs.astype(jnp.float32)
    mean = jnp.mean(values, axis=1, keepdims=True)
    center = values - mean
    inverse = lax.rsqrt(jnp.mean(center * center, axis=1, keepdims=True) + 1e-06)
    scaled = (center * inverse * ln_gain[None, :]).astype(jnp.bfloat16)
    pair = core_sum(
        lax.dot_general(
            scaled, query_grad, (((0,), (0,)), ((), ())), preferred_element_type=jnp.float32
        )
    )
    column = exchange(pair, "z_lo").astype(jnp.bfloat16)
    across, _ = lax.optimization_barrier((across, column))
    weight_grad = exchange(column, "y") / lax.axis_size(DP)

    halves = across.reshape(2, own_rows, features)
    me = lax.axis_index("z_hi")
    other = lax.dynamic_index_in_dim(halves, 1 - me, 0, False)
    own = lax.dynamic_index_in_dim(halves, me, 0, False)
    d_scaled = own.astype(jnp.float32) + shifted(other, "z_hi", 1).astype(jnp.float32)

    first = lax.axis_index(TENSOR) * own_rows
    own_values = lax.dynamic_slice_in_dim(inputs, first, own_rows, 0).astype(jnp.float32)
    mean_own = lax.dynamic_slice_in_dim(mean, first, own_rows, 0)
    inverse_own = lax.dynamic_slice_in_dim(inverse, first, own_rows, 0)
    normed_own = (own_values - mean_own) * inverse_own
    gated = d_scaled * ln_gain[None, :]
    mean_g = jnp.mean(gated, axis=1, keepdims=True)
    mean_gn = jnp.mean(gated * normed_own, axis=1, keepdims=True)
    input_grad = skip_grad.astype(jnp.float32) + inverse_own * (
        gated - mean_g - normed_own * mean_gn
    )
    return (input_grad.astype(jnp.bfloat16), weight_grad)


def solution(mesh):
    fine = Mesh(mesh.devices.reshape(SPLIT), DP + TENSOR)
    placed = (P(DP, None), P(), P(None, TENSOR), P(DP, TENSOR), P(DP + TENSOR, None))
    return jax.shard_map(
        per_device,
        mesh=fine,
        in_specs=placed,
        out_specs=(P(DP + TENSOR, None), P(DP, TENSOR)),
        check_vma=False,
    )
```

```python
import jax
import jax.numpy as jnp
from jax import lax
from jax.sharding import Mesh, PartitionSpec as P

DP = ("y", "z_lo", "core")
TENSOR = ("x", "z_hi")
SPLIT = (8, 4, 2, 8, 2)


def wide(part):
    return part.astype(jnp.float32)


def narrow(part):
    return part.astype(jnp.bfloat16)


def swap(part, axis, bit):
    return lax.ppermute(part, axis, [(i, i ^ bit) for i in range(lax.axis_size(axis))])


def swap_even(part, axis):
    return swap(part, axis, 1)


def swap_odd(part, axis):
    size = lax.axis_size(axis)
    return lax.ppermute(
        part, axis, [(i, (i + 1 if i % 2 else i - 1) % size) for i in range(size)]
    )


def pair_blocks(term):
    cores, rows = lax.axis_size("core"), term.shape[0] // lax.axis_size(DP)
    return term.reshape(-1, cores, rows, term.shape[1])


def core_half(blocks, index):
    return lax.dynamic_index_in_dim(blocks, index, 1, False)


def weight_reduce(pair):
    parts = lax.all_to_all(pair, ("y", "z_lo"), 0, 0, tiled=True)
    return jnp.sum(wide(parts), axis=0) / lax.axis_size(DP)


def product(query_grad, w_query):
    return narrow(
        lax.dot_general(
            query_grad, w_query, (((1,), (1,)), ((), ())), preferred_element_type=jnp.float32
        )
    )


def pick(parts, index):
    return lax.dynamic_index_in_dim(parts, index, 0, False)


def per_device(inputs, ln_gain, w_query, query_grad, skip_grad):
    size, sets = lax.axis_size("x"), lax.axis_size("z_hi")
    far = size // 2
    own_rows = skip_grad.shape[0]
    x, z_hi, core = lax.axis_index("x"), lax.axis_index("z_hi"), lax.axis_index("core")
    parity = x % 2
    way = 1 - 2 * parity
    chunk_rows = sets * own_rows
    chunk = lax.dynamic_slice_in_dim(query_grad, (x + far) % size * chunk_rows, chunk_rows, 0)
    farthest = product(chunk, w_query).reshape(sets, own_rows, -1)
    farthest, query_grad, inputs = lax.optimization_barrier((farthest, query_grad, inputs))
    one = swap_even(pick(farthest, parity), "x")
    two = swap_odd(pick(farthest, 1 - parity), "x")

    terms = product(query_grad, w_query).reshape(size, sets, own_rows, -1)
    values = wide(inputs)
    mean = jnp.mean(values, axis=1, keepdims=True)

    def term(step):
        return pick(terms, (x + step + size) % size)

    which = jnp.arange(sets)[:, None, None]
    one = jnp.where(which == 1 - parity, one[None], jnp.bfloat16(0))
    two = jnp.where(which == parity, two[None], jnp.bfloat16(0))
    up = narrow(wide(term(way * (far - 1))) + wide(two))
    down = narrow(wide(term(-way * (far - 1))) + wide(one))
    up, down, mean = lax.optimization_barrier((up, down, mean))
    one, two = swap_even(up, "x"), swap_odd(down, "x")

    center = values - mean
    inverse = lax.rsqrt(jnp.mean(center * center, axis=1, keepdims=True) + 1e-06)
    scaled = narrow(center * inverse * ln_gain[None, :])
    blocks = pair_blocks(
        narrow(
            lax.dot_general(
                scaled, query_grad, (((0,), (0,)), ((), ())), preferred_element_type=jnp.float32
            )
        )
    )
    received = swap(core_half(blocks, 1 - core), "core", 1)
    pair = narrow(wide(core_half(blocks, core)) + wide(received))
    one, two, _ = lax.optimization_barrier((one, two, pair))
    up = narrow(wide(term(way * 2)) + wide(two))
    down = narrow(wide(term(-way * 2)) + wide(one))
    up, down = lax.optimization_barrier((up, down))
    one, two = swap_even(up, "x"), swap_odd(down, "x")

    weight_grad = weight_reduce(pair)
    up = narrow(wide(term(way)) + wide(two))
    down = narrow(wide(term(-way)) + wide(one))
    up, down = lax.optimization_barrier((up, down))
    one, two = swap_even(up, "x"), swap_odd(down, "x")

    def total(index):
        return wide(pick(term(0), index)) + wide(pick(one, index)) + wide(pick(two, index))

    d_scaled = total(z_hi) + wide(swap(narrow(total(1 - z_hi)), "z_hi", 1))

    first = lax.axis_index(TENSOR) * own_rows
    own_values = lax.dynamic_slice_in_dim(inputs, first, own_rows, 0).astype(jnp.float32)
    mean_own = lax.dynamic_slice_in_dim(mean, first, own_rows, 0)
    inverse_own = lax.dynamic_slice_in_dim(inverse, first, own_rows, 0)
    normed_own = (own_values - mean_own) * inverse_own
    gated = d_scaled * ln_gain[None, :]
    mean_g = jnp.mean(gated, axis=1, keepdims=True)
    mean_gn = jnp.mean(gated * normed_own, axis=1, keepdims=True)
    input_grad = skip_grad.astype(jnp.float32) + inverse_own * (
        gated - mean_g - normed_own * mean_gn
    )
    return (input_grad.astype(jnp.bfloat16), weight_grad)


def solution(mesh):
    fine = Mesh(mesh.devices.reshape(SPLIT), DP + TENSOR)
    placed = (P(DP, None), P(), P(None, TENSOR), P(DP, TENSOR), P(DP + TENSOR, None))
    return jax.shard_map(
        per_device,
        mesh=fine,
        in_specs=placed,
        out_specs=(P(DP + TENSOR, None), P(DP, TENSOR)),
        check_vma=False,
    )
```

```python
import jax
import jax.numpy as jnp
from jax import lax
from jax.experimental import pallas as pl
from jax.experimental.pallas import tpu as pltpu
from jax.sharding import Mesh, PartitionSpec as P

DP = ("y", "z_lo", "core")
TENSOR = ("x", "z_hi")
SPLIT = (8, 4, 2, 8, 2)


def shifted(part, axis, step):
    size = lax.axis_size(axis)
    return lax.ppermute(part, axis, [(i, (i + step) % size) for i in range(size)])


def core_sum(term):
    rows, columns = term.shape[0] // lax.axis_size(DP), term.shape[1]
    sizes = [lax.axis_size(axis) for axis in DP]
    blocks = term.astype(jnp.bfloat16).reshape(*sizes, rows, columns)
    me = lax.axis_index("core")
    own = lax.dynamic_index_in_dim(blocks, me, 2, False)
    other = lax.dynamic_index_in_dim(blocks, 1 - me, 2, False)
    pair = own.astype(jnp.float32) + shifted(other, "core", 1).astype(jnp.float32)
    return pair.astype(jnp.bfloat16).swapaxes(0, 1)


def exchange(total, axis):
    return jnp.sum(lax.all_to_all(total, axis, 0, 0, tiled=True).astype(jnp.float32), axis=0)


PIECES = 4


def product_kernel(grads_hbm, weights_hbm, out_hbm, grads, weights, out, took, loaded, stored):
    pieces, block = weights.shape[:2]
    first = pltpu.make_async_copy(grads_hbm, grads, took)
    first.start()
    loads = []
    for i in range(pieces):
        load = pltpu.make_async_copy(
            weights_hbm.at[pl.ds(i * block, block)], weights.at[i], loaded.at[i]
        )
        load.start()
        loads.append(load)
    first.wait()
    stores = []
    for i in range(pieces):
        loads[i].wait()
        out[i] = lax.dot_general(
            grads[...],
            weights[i],
            (((1,), (1,)), ((), ())),
            preferred_element_type=jnp.float32,
        ).astype(out.dtype)
        store = pltpu.make_async_copy(
            out.at[i], out_hbm.at[:, pl.ds(i * block, block)], stored.at[i]
        )
        store.start()
        stores.append(store)
    for store in stores:
        store.wait()


def product(query_grad, w_query, features):
    rows, depth = query_grad.shape
    block = features // PIECES
    return pl.pallas_call(
        product_kernel,
        in_specs=[pl.BlockSpec(memory_space=pl.ANY)] * 2,
        out_specs=pl.BlockSpec(memory_space=pl.ANY),
        out_shape=jax.ShapeDtypeStruct((rows, features), jnp.bfloat16),
        scratch_shapes=[
            pltpu.VMEM((rows, depth), jnp.bfloat16),
            pltpu.VMEM((PIECES, block, depth), jnp.bfloat16),
            pltpu.VMEM((PIECES, rows, block), jnp.bfloat16),
            pltpu.SemaphoreType.DMA,
            pltpu.SemaphoreType.DMA((PIECES,)),
            pltpu.SemaphoreType.DMA((PIECES,)),
        ],
        compiler_params=pltpu.CompilerParams(vmem_limit_bytes=60 << 20),
        cost_estimate=pl.CostEstimate(
            flops=2 * rows * depth * features,
            bytes_accessed=2 * (rows * depth + features * depth + rows * features),
            transcendentals=0,
        ),
    )(query_grad, w_query)


def finish_kernel(own_ref, arrived_ref, normed_ref, inverse_ref, skip_ref, gain_ref, out_ref):
    normed = normed_ref[...]
    summed = own_ref[...].astype(jnp.float32) + arrived_ref[...].astype(jnp.float32)
    gated = summed * gain_ref[...]
    mean_g = jnp.mean(gated, axis=1, keepdims=True)
    mean_gn = jnp.mean(gated * normed, axis=1, keepdims=True)
    grad = skip_ref[...].astype(jnp.float32) + inverse_ref[...] * (
        gated - mean_g - normed * mean_gn
    )
    out_ref[...] = grad.astype(out_ref.dtype)


def finish(own, arrived, normed, inverse, skip_grad, ln_gain):
    return pl.pallas_call(
        finish_kernel,
        in_specs=[pl.BlockSpec(memory_space=pltpu.VMEM)] * 6,
        out_specs=pl.BlockSpec(memory_space=pltpu.VMEM),
        out_shape=jax.ShapeDtypeStruct(skip_grad.shape, jnp.bfloat16),
        compiler_params=pltpu.CompilerParams(vmem_limit_bytes=16 << 20),
    )(own, arrived, normed, inverse, skip_grad, ln_gain[None, :])


def per_device(inputs, ln_gain, w_query, query_grad, skip_grad):
    own_rows, features = skip_grad.shape
    term = product(query_grad, w_query, features)
    across = lax.psum_scatter(term, "x", scatter_dimension=0, tiled=True)

    values = inputs.astype(jnp.float32)
    mean = jnp.mean(values, axis=1, keepdims=True)
    center = values - mean
    inverse = lax.rsqrt(jnp.mean(center * center, axis=1, keepdims=True) + 1e-06)
    scaled = (center * inverse * ln_gain[None, :]).astype(jnp.bfloat16)
    pair = core_sum(
        lax.dot_general(
            scaled, query_grad, (((0,), (0,)), ((), ())), preferred_element_type=jnp.float32
        )
    )
    column = exchange(pair, "z_lo").astype(jnp.bfloat16)
    across, _ = lax.optimization_barrier((across, column))
    weight_grad = exchange(column, "y") / lax.axis_size(DP)

    halves = across.reshape(2, own_rows, features)
    me = lax.axis_index("z_hi")
    other = lax.dynamic_index_in_dim(halves, 1 - me, 0, False)
    own = lax.dynamic_index_in_dim(halves, me, 0, False)
    arrived = shifted(other, "z_hi", 1)

    first = lax.axis_index(TENSOR) * own_rows
    own_values = lax.dynamic_slice_in_dim(inputs, first, own_rows, 0).astype(jnp.float32)
    mean_own = lax.dynamic_slice_in_dim(mean, first, own_rows, 0)
    inverse_own = lax.dynamic_slice_in_dim(inverse, first, own_rows, 0)
    normed_own = (own_values - mean_own) * inverse_own
    input_grad = finish(own, arrived, normed_own, inverse_own, skip_grad, ln_gain)
    return (input_grad, weight_grad)


def solution(mesh):
    fine = Mesh(mesh.devices.reshape(SPLIT), DP + TENSOR)
    placed = (P(DP, None), P(), P(None, TENSOR), P(DP, TENSOR), P(DP + TENSOR, None))
    return jax.shard_map(
        per_device,
        mesh=fine,
        in_specs=placed,
        out_specs=(P(DP + TENSOR, None), P(DP, TENSOR)),
        check_vma=False,
    )
```

```python
import jax
import jax.numpy as jnp
from jax import lax
from jax.experimental import pallas as pl
from jax.experimental.pallas import tpu as pltpu
from jax.sharding import Mesh, PartitionSpec as P

DP = ("y", "z_lo", "core")
TENSOR = ("x", "z_hi")
SPLIT = (8, 4, 2, 8, 2)


def shifted(part, axis, step):
    size = lax.axis_size(axis)
    return lax.ppermute(part, axis, [(i, (i + step) % size) for i in range(size)])


def core_sum(term):
    rows, columns = term.shape[0] // lax.axis_size(DP), term.shape[1]
    sizes = [lax.axis_size(axis) for axis in DP]
    blocks = term.astype(jnp.bfloat16).reshape(*sizes, rows, columns)
    me = lax.axis_index("core")
    own = lax.dynamic_index_in_dim(blocks, me, 2, False)
    other = lax.dynamic_index_in_dim(blocks, 1 - me, 2, False)
    pair = own.astype(jnp.float32) + shifted(other, "core", 1).astype(jnp.float32)
    return pair.astype(jnp.bfloat16).swapaxes(0, 1)


def exchange(total, axis):
    return jnp.sum(lax.all_to_all(total, axis, 0, 0, tiled=True).astype(jnp.float32), axis=0)


PIECES = 4


def product_kernel(grads_hbm, weights_hbm, out_hbm, grads, weights, out, took, loaded, stored):
    pieces, block = weights.shape[:2]
    first = pltpu.make_async_copy(grads_hbm, grads, took)
    first.start()
    loads = []
    for i in range(pieces):
        load = pltpu.make_async_copy(
            weights_hbm.at[pl.ds(i * block, block)], weights.at[i], loaded.at[i]
        )
        load.start()
        loads.append(load)
    first.wait()
    stores = []
    for i in range(pieces):
        loads[i].wait()
        out[i] = lax.dot_general(
            grads[...],
            weights[i],
            (((1,), (1,)), ((), ())),
            preferred_element_type=jnp.float32,
        ).astype(out.dtype)
        store = pltpu.make_async_copy(
            out.at[i], out_hbm.at[:, pl.ds(i * block, block)], stored.at[i]
        )
        store.start()
        stores.append(store)
    for store in stores:
        store.wait()


def product(query_grad, w_query, features):
    rows, depth = query_grad.shape
    block = features // PIECES
    return pl.pallas_call(
        product_kernel,
        in_specs=[pl.BlockSpec(memory_space=pl.ANY)] * 2,
        out_specs=pl.BlockSpec(memory_space=pl.ANY),
        out_shape=jax.ShapeDtypeStruct((rows, features), jnp.bfloat16),
        scratch_shapes=[
            pltpu.VMEM((rows, depth), jnp.bfloat16),
            pltpu.VMEM((PIECES, block, depth), jnp.bfloat16),
            pltpu.VMEM((PIECES, rows, block), jnp.bfloat16),
            pltpu.SemaphoreType.DMA,
            pltpu.SemaphoreType.DMA((PIECES,)),
            pltpu.SemaphoreType.DMA((PIECES,)),
        ],
        compiler_params=pltpu.CompilerParams(vmem_limit_bytes=60 << 20),
        cost_estimate=pl.CostEstimate(
            flops=2 * rows * depth * features,
            bytes_accessed=2 * (rows * depth + features * depth + rows * features),
            transcendentals=0,
        ),
    )(query_grad, w_query)


def scaled_kernel(inputs_ref, gain_ref, out_ref):
    values = inputs_ref[...].astype(jnp.float32)
    center = values - jnp.mean(values, axis=1, keepdims=True)
    inverse = lax.rsqrt(jnp.mean(center * center, axis=1, keepdims=True) + 1e-06)
    out_ref[...] = (center * inverse * gain_ref[...]).astype(out_ref.dtype)


def layer_norm(inputs, ln_gain):
    rows, features = inputs.shape
    block = rows // 6
    return pl.pallas_call(
        scaled_kernel,
        grid=(rows // block,),
        in_specs=[
            pl.BlockSpec((block, features), lambda i: (i, 0)),
            pl.BlockSpec((1, features), lambda i: (0, 0)),
        ],
        out_specs=pl.BlockSpec((block, features), lambda i: (i, 0)),
        out_shape=jax.ShapeDtypeStruct(inputs.shape, jnp.bfloat16),
        compiler_params=pltpu.CompilerParams(vmem_limit_bytes=60 << 20),
    )(inputs, ln_gain[None, :])


def finish_kernel(own_ref, arrived_ref, normed_ref, inverse_ref, skip_ref, gain_ref, out_ref):
    normed = normed_ref[...]
    summed = own_ref[...].astype(jnp.float32) + arrived_ref[...].astype(jnp.float32)
    gated = summed * gain_ref[...]
    mean_g = jnp.mean(gated, axis=1, keepdims=True)
    mean_gn = jnp.mean(gated * normed, axis=1, keepdims=True)
    grad = skip_ref[...].astype(jnp.float32) + inverse_ref[...] * (
        gated - mean_g - normed * mean_gn
    )
    out_ref[...] = grad.astype(out_ref.dtype)


def finish(own, arrived, normed, inverse, skip_grad, ln_gain):
    return pl.pallas_call(
        finish_kernel,
        in_specs=[pl.BlockSpec(memory_space=pltpu.VMEM)] * 6,
        out_specs=pl.BlockSpec(memory_space=pltpu.VMEM),
        out_shape=jax.ShapeDtypeStruct(skip_grad.shape, jnp.bfloat16),
        compiler_params=pltpu.CompilerParams(vmem_limit_bytes=16 << 20),
    )(own, arrived, normed, inverse, skip_grad, ln_gain[None, :])


def per_device(inputs, ln_gain, w_query, query_grad, skip_grad):
    own_rows, features = skip_grad.shape
    term = product(query_grad, w_query, features)
    across = lax.psum_scatter(term, "x", scatter_dimension=0, tiled=True)

    scaled = layer_norm(inputs, ln_gain)
    pair = core_sum(
        lax.dot_general(
            scaled, query_grad, (((0,), (0,)), ((), ())), preferred_element_type=jnp.float32
        )
    )
    column = exchange(pair, "z_lo").astype(jnp.bfloat16)
    across, _ = lax.optimization_barrier((across, column))
    weight_grad = exchange(column, "y") / lax.axis_size(DP)

    halves = across.reshape(2, own_rows, features)
    me = lax.axis_index("z_hi")
    other = lax.dynamic_index_in_dim(halves, 1 - me, 0, False)
    own = lax.dynamic_index_in_dim(halves, me, 0, False)
    arrived = shifted(other, "z_hi", 1)

    first = lax.axis_index(TENSOR) * own_rows
    inputs, _ = lax.optimization_barrier((inputs, pair))
    values = lax.dynamic_slice_in_dim(inputs, first, own_rows, 0).astype(jnp.float32)
    center = values - jnp.mean(values, axis=1, keepdims=True)
    inverse = lax.rsqrt(jnp.mean(center * center, axis=1, keepdims=True) + 1e-06)
    input_grad = finish(own, arrived, center * inverse, inverse, skip_grad, ln_gain)
    return (input_grad, weight_grad)


def solution(mesh):
    fine = Mesh(mesh.devices.reshape(SPLIT), DP + TENSOR)
    placed = (P(DP, None), P(), P(None, TENSOR), P(DP, TENSOR), P(DP + TENSOR, None))
    return jax.shard_map(
        per_device,
        mesh=fine,
        in_specs=placed,
        out_specs=(P(DP + TENSOR, None), P(DP, TENSOR)),
        check_vma=False,
    )
```

```python
import jax
import jax.numpy as jnp
from jax import lax
from jax.experimental import pallas as pl
from jax.experimental.pallas import tpu as pltpu
from jax.sharding import Mesh, PartitionSpec as P

DP = ("y", "z_lo", "core")
TENSOR = ("x", "z_hi")
SPLIT = (8, 4, 2, 8, 2)


def shifted(part, axis, step):
    size = lax.axis_size(axis)
    return lax.ppermute(part, axis, [(i, (i + step) % size) for i in range(size)])


def core_sum(term):
    rows, columns = term.shape[0] // lax.axis_size(DP), term.shape[1]
    blocks = term.astype(jnp.bfloat16).reshape(-1, lax.axis_size("core"), rows, columns)
    me = lax.axis_index("core")
    own = lax.dynamic_index_in_dim(blocks, me, 1, False)
    other = lax.dynamic_index_in_dim(blocks, 1 - me, 1, False)
    pair = own.astype(jnp.float32) + shifted(other, "core", 1).astype(jnp.float32)
    return pair.astype(jnp.bfloat16)


def exchange(total, axis):
    return jnp.sum(lax.all_to_all(total, axis, 0, 0, tiled=True).astype(jnp.float32), axis=0)


PIECES = 4


def product_kernel(grads_hbm, weights_hbm, out_hbm, grads, weights, out, took, loaded, stored):
    pieces, block = weights.shape[:2]
    first = pltpu.make_async_copy(grads_hbm, grads, took)
    first.start()
    loads = []
    for i in range(pieces):
        load = pltpu.make_async_copy(
            weights_hbm.at[pl.ds(i * block, block)], weights.at[i], loaded.at[i]
        )
        load.start()
        loads.append(load)
    first.wait()
    stores = []
    for i in range(pieces):
        loads[i].wait()
        out[i] = lax.dot_general(
            grads[...],
            weights[i],
            (((1,), (1,)), ((), ())),
            preferred_element_type=jnp.float32,
        ).astype(out.dtype)
        store = pltpu.make_async_copy(
            out.at[i], out_hbm.at[:, pl.ds(i * block, block)], stored.at[i]
        )
        store.start()
        stores.append(store)
    for store in stores:
        store.wait()


def product(query_grad, w_query, features):
    rows, depth = query_grad.shape
    block = features // PIECES
    return pl.pallas_call(
        product_kernel,
        in_specs=[pl.BlockSpec(memory_space=pl.ANY)] * 2,
        out_specs=pl.BlockSpec(memory_space=pl.ANY),
        out_shape=jax.ShapeDtypeStruct((rows, features), jnp.bfloat16),
        scratch_shapes=[
            pltpu.VMEM((rows, depth), jnp.bfloat16),
            pltpu.VMEM((PIECES, block, depth), jnp.bfloat16),
            pltpu.VMEM((PIECES, rows, block), jnp.bfloat16),
            pltpu.SemaphoreType.DMA,
            pltpu.SemaphoreType.DMA((PIECES,)),
            pltpu.SemaphoreType.DMA((PIECES,)),
        ],
        compiler_params=pltpu.CompilerParams(vmem_limit_bytes=60 << 20),
        cost_estimate=pl.CostEstimate(
            flops=2 * rows * depth * features,
            bytes_accessed=2 * (rows * depth + features * depth + rows * features),
            transcendentals=0,
        ),
    )(query_grad, w_query)


def finish_kernel(own_ref, arrived_ref, normed_ref, inverse_ref, skip_ref, gain_ref, out_ref):
    normed = normed_ref[...]
    summed = own_ref[...].astype(jnp.float32) + arrived_ref[...].astype(jnp.float32)
    gated = summed * gain_ref[...]
    mean_g = jnp.mean(gated, axis=1, keepdims=True)
    mean_gn = jnp.mean(gated * normed, axis=1, keepdims=True)
    grad = skip_ref[...].astype(jnp.float32) + inverse_ref[...] * (
        gated - mean_g - normed * mean_gn
    )
    out_ref[...] = grad.astype(out_ref.dtype)


def finish(own, arrived, normed, inverse, skip_grad, ln_gain):
    return pl.pallas_call(
        finish_kernel,
        in_specs=[pl.BlockSpec(memory_space=pltpu.VMEM)] * 6,
        out_specs=pl.BlockSpec(memory_space=pltpu.VMEM),
        out_shape=jax.ShapeDtypeStruct(skip_grad.shape, jnp.bfloat16),
        compiler_params=pltpu.CompilerParams(vmem_limit_bytes=16 << 20),
    )(own, arrived, normed, inverse, skip_grad, ln_gain[None, :])


def per_device(inputs, ln_gain, w_query, query_grad, skip_grad):
    own_rows, features = skip_grad.shape
    term = product(query_grad, w_query, features)
    across = lax.psum_scatter(term, "x", scatter_dimension=0, tiled=True)

    values = inputs.astype(jnp.float32)
    mean = jnp.mean(values, axis=1, keepdims=True)
    center = values - mean
    inverse = lax.rsqrt(jnp.mean(center * center, axis=1, keepdims=True) + 1e-06)
    scaled = (center * inverse * ln_gain[None, :]).astype(jnp.bfloat16)
    pair = core_sum(
        lax.dot_general(
            scaled, query_grad, (((0,), (0,)), ((), ())), preferred_element_type=jnp.float32
        )
    )
    weight_grad = exchange(pair, ("y", "z_lo")) / lax.axis_size(DP)

    halves = across.reshape(2, own_rows, features)
    me = lax.axis_index("z_hi")
    other = lax.dynamic_index_in_dim(halves, 1 - me, 0, False)
    own = lax.dynamic_index_in_dim(halves, me, 0, False)
    arrived = shifted(other, "z_hi", 1)

    first = lax.axis_index(TENSOR) * own_rows
    own_values = lax.dynamic_slice_in_dim(inputs, first, own_rows, 0).astype(jnp.float32)
    mean_own = lax.dynamic_slice_in_dim(mean, first, own_rows, 0)
    inverse_own = lax.dynamic_slice_in_dim(inverse, first, own_rows, 0)
    normed_own = (own_values - mean_own) * inverse_own
    input_grad = finish(own, arrived, normed_own, inverse_own, skip_grad, ln_gain)
    return (input_grad, weight_grad)


def solution(mesh):
    fine = Mesh(mesh.devices.reshape(SPLIT), DP + TENSOR)
    placed = (P(DP, None), P(), P(None, TENSOR), P(DP, TENSOR), P(DP + TENSOR, None))
    return jax.shard_map(
        per_device,
        mesh=fine,
        in_specs=placed,
        out_specs=(P(DP + TENSOR, None), P(DP, TENSOR)),
        check_vma=False,
    )
```

```python
import jax
import jax.numpy as jnp
from jax import lax
from jax.experimental import pallas as pl
from jax.experimental.pallas import tpu as pltpu
from jax.sharding import Mesh, PartitionSpec as P

DP = ("y", "z_lo", "core")
TENSOR = ("x", "z_hi")
SPLIT = (8, 4, 2, 8, 2)


def shifted(part, axis, step):
    size = lax.axis_size(axis)
    return lax.ppermute(part, axis, [(i, (i + step) % size) for i in range(size)])


def core_sum(term):
    rows, columns = term.shape[0] // lax.axis_size(DP), term.shape[1]
    blocks = term.astype(jnp.bfloat16).reshape(-1, lax.axis_size("core"), rows, columns)
    me = lax.axis_index("core")
    own = lax.dynamic_index_in_dim(blocks, me, 1, False)
    other = lax.dynamic_index_in_dim(blocks, 1 - me, 1, False)
    pair = own.astype(jnp.float32) + shifted(other, "core", 1).astype(jnp.float32)
    return pair.astype(jnp.bfloat16)


def exchange(total, axis):
    return jnp.sum(lax.all_to_all(total, axis, 0, 0, tiled=True).astype(jnp.float32), axis=0)


PIECES = 3


def product_kernel(grads_hbm, weights_hbm, out_hbm, grads, weights, out, took, loaded, stored):
    pieces, block = weights.shape[:2]
    first = pltpu.make_async_copy(grads_hbm, grads, took)
    first.start()
    loads = []
    for i in range(pieces):
        load = pltpu.make_async_copy(
            weights_hbm.at[pl.ds(i * block, block)], weights.at[i], loaded.at[i]
        )
        load.start()
        loads.append(load)
    first.wait()
    stores = []
    for i in range(pieces):
        loads[i].wait()
        out[i] = lax.dot_general(
            grads[...],
            weights[i],
            (((1,), (1,)), ((), ())),
            preferred_element_type=jnp.float32,
        ).astype(out.dtype)
        store = pltpu.make_async_copy(
            out.at[i], out_hbm.at[:, pl.ds(i * block, block)], stored.at[i]
        )
        store.start()
        stores.append(store)
    for store in stores:
        store.wait()


def product(query_grad, w_query, features):
    rows, depth = query_grad.shape
    block = features // PIECES
    return pl.pallas_call(
        product_kernel,
        in_specs=[pl.BlockSpec(memory_space=pl.ANY)] * 2,
        out_specs=pl.BlockSpec(memory_space=pl.ANY),
        out_shape=jax.ShapeDtypeStruct((rows, features), jnp.bfloat16),
        scratch_shapes=[
            pltpu.VMEM((rows, depth), jnp.bfloat16),
            pltpu.VMEM((PIECES, block, depth), jnp.bfloat16),
            pltpu.VMEM((PIECES, rows, block), jnp.bfloat16),
            pltpu.SemaphoreType.DMA,
            pltpu.SemaphoreType.DMA((PIECES,)),
            pltpu.SemaphoreType.DMA((PIECES,)),
        ],
        compiler_params=pltpu.CompilerParams(vmem_limit_bytes=60 << 20),
        cost_estimate=pl.CostEstimate(
            flops=2 * rows * depth * features,
            bytes_accessed=2 * (rows * depth + features * depth + rows * features),
            transcendentals=0,
        ),
    )(query_grad, w_query)


def finish_kernel(own_ref, arrived_ref, normed_ref, inverse_ref, skip_ref, gain_ref, out_ref):
    normed = normed_ref[...]
    summed = own_ref[...].astype(jnp.float32) + arrived_ref[...].astype(jnp.float32)
    gated = summed * gain_ref[...]
    mean_g = jnp.mean(gated, axis=1, keepdims=True)
    mean_gn = jnp.mean(gated * normed, axis=1, keepdims=True)
    grad = skip_ref[...].astype(jnp.float32) + inverse_ref[...] * (
        gated - mean_g - normed * mean_gn
    )
    out_ref[...] = grad.astype(out_ref.dtype)


def finish(own, arrived, normed, inverse, skip_grad, ln_gain):
    return pl.pallas_call(
        finish_kernel,
        in_specs=[pl.BlockSpec(memory_space=pltpu.VMEM)] * 6,
        out_specs=pl.BlockSpec(memory_space=pltpu.VMEM),
        out_shape=jax.ShapeDtypeStruct(skip_grad.shape, jnp.bfloat16),
        compiler_params=pltpu.CompilerParams(vmem_limit_bytes=16 << 20),
    )(own, arrived, normed, inverse, skip_grad, ln_gain[None, :])


def per_device(inputs, ln_gain, w_query, query_grad, skip_grad):
    own_rows, features = skip_grad.shape
    term = product(query_grad, w_query, features)
    across = lax.psum_scatter(term, "x", scatter_dimension=0, tiled=True)

    values = inputs.astype(jnp.float32)
    mean = jnp.mean(values, axis=1, keepdims=True)
    center = values - mean
    inverse = lax.rsqrt(jnp.mean(center * center, axis=1, keepdims=True) + 1e-06)
    scaled = (center * inverse * ln_gain[None, :]).astype(jnp.bfloat16)
    pair = core_sum(
        lax.dot_general(
            scaled, query_grad, (((0,), (0,)), ((), ())), preferred_element_type=jnp.float32
        )
    )
    weight_grad = exchange(pair, ("y", "z_lo")) / lax.axis_size(DP)

    halves = across.reshape(2, own_rows, features)
    me = lax.axis_index("z_hi")
    other = lax.dynamic_index_in_dim(halves, 1 - me, 0, False)
    own = lax.dynamic_index_in_dim(halves, me, 0, False)
    arrived = shifted(other, "z_hi", 1)

    first = lax.axis_index(TENSOR) * own_rows
    own_values = lax.dynamic_slice_in_dim(inputs, first, own_rows, 0).astype(jnp.float32)
    mean_own = lax.dynamic_slice_in_dim(mean, first, own_rows, 0)
    inverse_own = lax.dynamic_slice_in_dim(inverse, first, own_rows, 0)
    normed_own = (own_values - mean_own) * inverse_own
    input_grad = finish(own, arrived, normed_own, inverse_own, skip_grad, ln_gain)
    return (input_grad, weight_grad)


def solution(mesh):
    fine = Mesh(mesh.devices.reshape(SPLIT), DP + TENSOR)
    placed = (P(DP, None), P(), P(None, TENSOR), P(DP, TENSOR), P(DP + TENSOR, None))
    return jax.shard_map(
        per_device,
        mesh=fine,
        in_specs=placed,
        out_specs=(P(DP + TENSOR, None), P(DP, TENSOR)),
        check_vma=False,
    )
```
